256 devices in a mesh: slab: 64 (over y_lo, x, z), ang: 4 (over y_hi, core).
Axes of the slice: x: 4, y: 4 (y_hi: 2, y_lo: 2; y = y_hi * 2 + y_lo), z: 8, core: 2. Of those that a mesh axis runs over, the one named last changes fastest.
Arguments:
- volume: float32 [256, 128, 4096], P('slab', 'ang'), may hold values from -6 to 6
- measured: float32 [16, 4096, 4096], P('ang', 'slab'), may hold values from -6 to 6
- incidence: int32 [16, 64, 5], P('ang', 'slab'), may hold values 0 or 1
- row_weights: float32 [16, 5, 4, 64], P('ang'), may hold values from -1.25 to 1.25
- path_table: float32 [2048, 128], P(None, 'ang'), may hold values from -0.5 to 0.5
- subset: int32 [16], replicated, may hold values from 0 to 2047
- gain_map: int32 [64, 64], P('slab'), may hold values from 0 to 4095
- gain_values: float32 [4096], replicated, may hold values from 0.5 to 1.5
Outputs:
- volume_next: float32 [256, 128, 4096], P('slab', 'ang')
- gain_next: float32 [4096], replicated
The draws below stay inside these ranges and needn't reach their ends.
All inputs are finite; a program needn't handle non-finite values. No bound on the sum of `incidence` on one device may be relied on, other than what follows from the above.
Results may differ from the reference program's by a relative error of at most 0.0003.
Values sent between devices are 32-bit elements; how exact they have to be, the bound alone decides.
No kernel may reach another device: no remote copies, remote signals or barrier semaphores. Data moves between devices by JAX's collectives and lax.ppermute only.
A program may use at most 64 MiB of HBM per device.

```python
import jax
import jax.numpy as jnp
from jax import lax

DETECTOR_COLUMNS = 4096
GAIN_BLOCK_SIZE = 64
NG = 4096
NALL = 2048
ZD = 4
REACH = 2
SUBSET_ANGLES = 16
SLAB_COUNT = 64
NZ = 256
XV = 128
NR = 4096
UB = 64


def touch_ends(result, own_key, least, high):
    extent = result.shape
    spot = [jax.random.randint(jax.random.fold_in(own_key, axis), (), 0, extent[axis]) for axis in range(len(extent))]
    result = result.at[tuple(spot)].set(least)
    longest = extent.index(max(extent))
    spot[longest] = (spot[longest] + 1) % extent[longest]
    return result.at[tuple(spot)].set(high)


def level_of(key, extent, shards, low, high):
    level, own = 1.0, jax.random.fold_in(key, 6)
    for position, parts in shards:
        heights = jnp.exp(jax.random.uniform(jax.random.fold_in(own, position), (parts,), jnp.float32, low / len(shards), high / len(shards)))
        level = level * jnp.repeat(heights, extent[position] // parts).reshape([-1 if axis == position else 1 for axis in range(len(extent))])
    return level


def bell_draw(key, dims, width, limit, split=(), kind=jnp.bfloat16):
    drawn = jax.random.normal(key, dims, jnp.float32) * width
    if len(split) > 0:
        drawn = level_of(key, dims, split, -0.22, 0.18) * drawn
    return jnp.clip(drawn, min=-limit, max=limit).astype(kind)


def setup_inputs(seed: int = 0) -> dict:
    seeds = jax.random.split(jax.random.key(seed), 9)
    volume = bell_draw(seeds[0], (NZ, XV, DETECTOR_COLUMNS), 1.0, 6.0, ((0, 64), (1, 4)), jnp.float32)
    measured = bell_draw(seeds[1], (SUBSET_ANGLES, NR, DETECTOR_COLUMNS), 1.0, 6.0, ((0, 4), (1, 64)), jnp.float32)
    incidence = touch_ends((jax.random.randint(seeds[2], (SUBSET_ANGLES, SLAB_COUNT, 2 * REACH + 1), 0, 4) < 3).astype(jnp.int32), jax.random.fold_in(seeds[2], 1), 0, 1)
    row_weights = bell_draw(seeds[3], (SUBSET_ANGLES, 2 * REACH + 1, ZD, GAIN_BLOCK_SIZE), (ZD * (2 * REACH + 1)) ** -0.5, 1.25, ((0, 4),), jnp.float32)
    path_table = bell_draw(seeds[4], (NALL, XV), XV ** -0.5, 0.5, ((1, 4),), jnp.float32)
    subset = touch_ends(jax.random.randint(seeds[5], (SUBSET_ANGLES,), 0, NALL), jax.random.fold_in(seeds[5], 1), 0, NALL - 1).astype(jnp.int32)
    gain_map = touch_ends(jax.random.randint(seeds[6], (SLAB_COUNT, UB), 0, NG), jax.random.fold_in(seeds[6], 1), 0, NG - 1).astype(jnp.int32)
    gain_values = jnp.clip(1.0 + 0.1 * jax.random.normal(seeds[7], (NG,), jnp.float32), 0.5, 1.5)
    return {"volume": volume, "measured": measured, "incidence": incidence, "row_weights": row_weights, "path_table": path_table, "subset": subset, "gain_map": gain_map, "gain_values": gain_values}


HIGH = lax.Precision.HIGHEST

def tv_from_padded(padded):
    lower = padded[:-1]
    diff_z = padded[1:] - lower
    diff_u = jnp.concatenate([lower[..., 1:], jnp.zeros_like(lower[..., :1])], axis=-1) - lower
    magnitude = jnp.sqrt(diff_z * diff_z + diff_u * diff_u + 0.25)
    flux_z = diff_z / magnitude
    flux_u = diff_u / magnitude
    moved_u = jnp.concatenate([jnp.zeros_like(flux_u[..., :1]), flux_u[..., :-1]], axis=-1)
    return flux_z[:-1] - flux_z[1:] + moved_u[1:] - flux_u[1:]

def reference(volume, measured, incidence, row_weights, path_table, subset, gain_map, gain_values):
    weights = path_table[subset]
    lines = jnp.einsum('ax,zxu->azu', weights, volume, precision=HIGH)
    lines = lines.reshape(SUBSET_ANGLES, SLAB_COUNT, ZD, DETECTOR_COLUMNS)
    padded = jnp.pad(lines, ((0, 0), (REACH, REACH), (0, 0), (0, 0)))
    forward_projection = jnp.zeros((SUBSET_ANGLES, SLAB_COUNT, GAIN_BLOCK_SIZE, DETECTOR_COLUMNS), jnp.float32)
    for offset in range(2 * REACH + 1):
        mask = incidence[:, :, offset].astype(jnp.float32)[:, :, None, None]
        forward_projection = forward_projection + mask * jnp.einsum('azr,abzu->abru', row_weights[:, offset], padded[:, offset:offset + SLAB_COUNT], precision=HIGH)
    measured_counts = measured.reshape(SUBSET_ANGLES, SLAB_COUNT, GAIN_BLOCK_SIZE, DETECTOR_COLUMNS)
    detector_pixel_gain = jnp.repeat(gain_values[gain_map], GAIN_BLOCK_SIZE, axis=1)[None, :, None, :]
    projection_residual = detector_pixel_gain * forward_projection - measured_counts
    weighted = detector_pixel_gain * projection_residual
    cross = (projection_residual * forward_projection).reshape(SUBSET_ANGLES, SLAB_COUNT, GAIN_BLOCK_SIZE, UB, GAIN_BLOCK_SIZE).sum(axis=(0, 2, 4))
    energy = (forward_projection * forward_projection).reshape(SUBSET_ANGLES, SLAB_COUNT, GAIN_BLOCK_SIZE, UB, GAIN_BLOCK_SIZE).sum(axis=(0, 2, 4))
    cross_sum = jax.ops.segment_sum(cross.reshape(-1), gain_map.reshape(-1), num_segments=NG)
    energy_sum = jax.ops.segment_sum(energy.reshape(-1), gain_map.reshape(-1), num_segments=NG)
    gain_next = gain_values - cross_sum / (energy_sum + 1.0)
    grads = jnp.zeros((SUBSET_ANGLES, SLAB_COUNT + 2 * REACH, ZD, DETECTOR_COLUMNS), jnp.float32)
    for offset in range(2 * REACH + 1):
        mask = incidence[:, :, offset].astype(jnp.float32)[:, :, None, None]
        part = jnp.einsum('azr,abru->abzu', row_weights[:, offset], weighted, precision=HIGH) * mask
        grads = grads.at[:, offset:offset + SLAB_COUNT].add(part)
    images = grads[:, REACH:REACH + SLAB_COUNT].reshape(SUBSET_ANGLES, NZ, DETECTOR_COLUMNS)
    gradient = jnp.einsum('ax,azu->zxu', weights, images, precision=HIGH)
    smooth = tv_from_padded(jnp.pad(volume, ((1, 1), (0, 0), (0, 0))))
    volume_next = volume - 0.2 * gradient - 0.2 * smooth
    return (volume_next, gain_next)
```

```python
import functools

import jax
import jax.numpy as jnp
from jax import lax
from jax.experimental import pallas as pl
from jax.experimental.pallas import tpu as pltpu
from jax.sharding import PartitionSpec as P

F32 = jnp.float32
BF16 = jnp.bfloat16
MIB = 1024 * 1024
LINES_LIMIT = 50


def split(value):
    high = value.astype(BF16)
    low = (value - high.astype(F32)).astype(BF16)
    return high, low


def params(limit=12):
    return pltpu.CompilerParams(vmem_limit_bytes=limit * MIB)


def cost(flops, moved):
    return pl.CostEstimate(flops=flops, bytes_accessed=moved, transcendentals=0)


def full(shape):
    return pl.BlockSpec(shape, lambda i: (0,) * len(shape))


def heading():
    return 1 - 2 * (lax.axis_index("ang") & 1)


def order_of(offsets):
    reach = offsets // 2
    ahead = heading()
    return (reach - ahead, reach + ahead, reach - 2 * ahead, reach + 2 * ahead, reach)


def lines_kernel(steps, subset_in, table_in, volume, *rest):
    outs, weights_out, leading, trailing = rest[:4], rest[4], rest[5], rest[6]
    held, table, subset, sems = rest[7:]
    planes, depth, columns = held.shape
    width = columns // steps
    groups = 4
    angles = weights_out.shape[0] // planes
    each = angles // groups

    def copy(step):
        run = pl.ds(step * width, width)
        return pltpu.make_async_copy(
            volume.at[:, :, run], held.at[:, :, run], sems.at[step]
        )

    subset_copy = pltpu.make_async_copy(subset_in, subset, sems.at[steps])
    table_copy = pltpu.make_async_copy(table_in, table, sems.at[steps + 1])
    subset_copy.start()
    table_copy.start()
    for step in range(steps):
        copy(step).start()

    subset_copy.wait()
    me = lax.axis_index("ang")
    slot = lax.broadcasted_iota(jnp.int32, (angles, 1), 0)
    wanted = jnp.zeros((angles, 1), jnp.int32)
    for group, owner in enumerate((3 - me, me ^ 1, me ^ 2, me)):
        for i in range(each):
            wanted = jnp.where(slot == group * each + i, subset[owner * each + i], wanted)
    entries = table.shape[1]
    onehot = jnp.where(
        lax.broadcasted_iota(jnp.int32, (angles, entries), 1) == wanted, 1.0, 0.0
    ).astype(BF16)
    picked = jnp.zeros((angles, depth), F32)
    table_copy.wait()
    rest_of = table[...]
    for _ in range(3):
        part = rest_of.astype(BF16)
        picked = picked + lax.dot_general(
            onehot, part, (((1,), (1,)), ((), ())), preferred_element_type=F32
        )
        rest_of = rest_of - part.astype(F32)
    wide = jnp.concatenate([picked] * planes, axis=1)
    mask = (
        lax.broadcasted_iota(jnp.int32, (planes, planes * depth), 0)
        == lax.broadcasted_iota(jnp.int32, (planes, planes * depth), 1) // depth
    )
    for angle in range(angles):
        row = jnp.broadcast_to(wide[angle : angle + 1], mask.shape)
        weights_out[angle * planes : (angle + 1) * planes, :] = jnp.where(mask, row, 0.0)
    high_w, low_w = split(weights_out[...])
    both_w = jnp.concatenate([high_w, low_w], axis=0)
    count = angles * planes
    size = count // groups
    first = jnp.where(heading() > 0, planes - 1, 0)
    for step in range(steps):
        copy(step).wait()
        run = slice(step * width, (step + 1) * width)
        leading[:, run] = held[first, :, run]
        trailing[:, run] = held[planes - 1 - first, :, run]
        high, low = split(held[:, :, run].reshape(planes * depth, width))
        main = jnp.dot(both_w, high, preferred_element_type=F32)
        lines = (
            main[:count]
            + main[count:]
            + jnp.dot(high_w, low, preferred_element_type=F32)
        )
        for group in range(groups):
            outs[group][:, run] = lines[group * size : (group + 1) * size]


def make_lines(subset, path_table, volume, steps=4):
    planes, depth, columns = volume.shape
    angles = subset.shape[0]
    rows = angles * planes // 4
    vmem = pl.BlockSpec(memory_space=pltpu.VMEM)
    return pl.pallas_call(
        functools.partial(lines_kernel, steps),
        in_specs=[pl.BlockSpec(memory_space=pl.ANY)] * 3,
        out_specs=[vmem] * 7,
        out_shape=[jax.ShapeDtypeStruct((rows, columns), F32)] * 4
        + [jax.ShapeDtypeStruct((angles * planes, planes * depth), F32)]
        + [jax.ShapeDtypeStruct((depth, columns), F32)] * 2,
        scratch_shapes=[
            pltpu.VMEM((planes, depth, columns), F32),
            pltpu.VMEM(path_table.shape[::-1], F32),
            pltpu.SMEM(subset.shape, jnp.int32),
            pltpu.SemaphoreType.DMA((steps + 2,)),
        ],
        compiler_params=params(LINES_LIMIT),
        cost_estimate=cost(6 * angles * planes * depth * columns, 3 * MIB),
        name="lines",
    )(subset, path_table.T, volume)


def add_kernel(count, *refs):
    total = refs[0][...]
    for ref in refs[1:count]:
        total = total + ref[...]
    out = refs[-1]
    out[...] = total


def add_through_kernel(count, passed, *refs):
    add_kernel(count, *refs[: len(refs) - passed])


def add(*values, after=(), through=()):
    vmem = pl.BlockSpec(memory_space=pltpu.VMEM)
    anywhere = pl.BlockSpec(memory_space=pl.ANY)
    count = len(values) + len(after)
    outs = pl.pallas_call(
        functools.partial(add_through_kernel, len(values), len(through)),
        in_specs=[vmem] * len(values) + [anywhere] * (len(after) + len(through)),
        out_specs=[vmem] + [anywhere] * len(through),
        out_shape=[jax.ShapeDtypeStruct(values[0].shape, F32)]
        + [jax.ShapeDtypeStruct(value.shape, value.dtype) for value in through],
        input_output_aliases={count + i: 1 + i for i in range(len(through))},
        compiler_params=params(8),
        cost_estimate=cost(values[0].size * len(values), values[0].size * 4 * len(values)),
        name="add",
    )(*values, *after, *through)
    return outs if through else outs[0]


def prepare_kernel(slabs, incidence, row_weights, gain_map, gain_values, *rest):
    ahead, back, gains, onehot = rest[-6:-2]
    flat = rest[-1]
    angles, offsets, planes, block = row_weights.shape
    flat[...] = jnp.zeros_like(flat)
    slab = lax.axis_index("slab")
    for spot, offset in enumerate(order_of(offsets)):
        other = slab + offset - offsets // 2
        inside = jnp.where((other >= 0) & (other < slabs), 1, 0)
        for angle in range(angles):
            factor = (incidence[angle, 0, offset] * inside).astype(F32)
            at = (spot * angles + angle) * planes
            flat[at : at + planes, angle * block : (angle + 1) * block] = (
                row_weights[angle, offset] * factor
            )
    high, low = split(flat[...])
    back[...] = jnp.concatenate([high, low], axis=0)
    turned = flat[...].T
    high, low = split(turned)
    ahead[...] = jnp.concatenate([high, low, high], axis=1)
    lane = lax.broadcasted_iota(jnp.int32, (1, 2 * block), 1)
    first = lane < block
    spot = lane & (block - 1)
    blocks = gain_map.shape[1]
    for i in range(blocks // 2):
        low_gain = gain_values[gain_map[0, 2 * i]]
        high_gain = gain_values[gain_map[0, 2 * i + 1]]
        gains[:, 2 * i * block : 2 * (i + 1) * block] = jnp.where(first, low_gain, high_gain)
    for i in range(blocks):
        index = gain_map[0, i]
        target = jnp.where(first, index // block, index & (block - 1))
        onehot[i : i + 1, :] = (spot == target).astype(F32)


def prepare(incidence, row_weights, gain_map, gain_values, slabs, after, through):
    angles, offsets, planes, block = row_weights.shape
    rows = offsets * angles * planes
    columns = gain_map.shape[1] * block
    smem = pl.BlockSpec(memory_space=pltpu.SMEM)
    anywhere = pl.BlockSpec(memory_space=pl.ANY)
    vmem = pl.BlockSpec(memory_space=pltpu.VMEM)
    return pl.pallas_call(
        functools.partial(prepare_kernel, slabs),
        in_specs=[smem, vmem, smem, smem] + [anywhere] * (len(after) + 1),
        out_specs=[vmem] * 4 + [anywhere],
        out_shape=[
            jax.ShapeDtypeStruct((angles * block, 3 * rows), BF16),
            jax.ShapeDtypeStruct((2 * rows, angles * block), BF16),
            jax.ShapeDtypeStruct((1, columns), F32),
            jax.ShapeDtypeStruct((gain_map.shape[1], 2 * block), F32),
            jax.ShapeDtypeStruct(through.shape, F32),
        ],
        input_output_aliases={4 + len(after): 4},
        scratch_shapes=[pltpu.VMEM((rows, angles * block), F32)],
        compiler_params=params(),
        cost_estimate=cost(1000000, 1 * MIB),
        name="prepare",
    )(incidence, row_weights, gain_map, gain_values, *after, through)


def detector_kernel(offsets, ahead, back, gains, measured, *refs):
    lines = refs[:offsets]
    outs = refs[-1 - offsets : -1]
    sums = refs[-1]
    angles, block, width = measured.shape
    high, low = split(jnp.concatenate([line[...] for line in lines], axis=0))
    stacked = jnp.concatenate([high, high, low], axis=0)
    forward = jnp.dot(ahead[...], stacked, preferred_element_type=F32)
    gain = gains[...]
    residual = gain * forward - measured[...].reshape(angles * block, width)
    weighted = gain * residual
    cross = jnp.sum(residual * forward, axis=0, keepdims=True)
    energy = jnp.sum(forward * forward, axis=0, keepdims=True)
    sums[...] = jnp.concatenate([cross, energy], axis=0)
    high, low = split(weighted)
    count = back.shape[0] // 2
    main = jnp.dot(back[...], high, preferred_element_type=F32)
    planes = (
        main[:count] + main[count:] + jnp.dot(back[:count], low, preferred_element_type=F32)
    )
    size = count // offsets
    for offset in range(offsets):
        outs[offset][...] = planes[offset * size : (offset + 1) * size]


def detector(ahead, back, gains, measured, lines, after=(), steps=8):
    offsets = len(lines)
    angles, block, columns = measured.shape
    rows = lines[0].shape[0]
    width = columns // steps
    piece = pl.BlockSpec((rows, width), lambda i: (0, i))
    return pl.pallas_call(
        functools.partial(detector_kernel, offsets),
        grid=(steps,),
        in_specs=[
            full(ahead.shape),
            full(back.shape),
            pl.BlockSpec((1, width), lambda i: (0, i)),
            pl.BlockSpec((angles, block, width), lambda i: (0, 0, i)),
        ]
        + [piece] * offsets
        + [pl.BlockSpec(memory_space=pl.ANY)] * len(after),
        out_specs=[piece] * offsets + [pl.BlockSpec((2, width), lambda i: (0, i))],
        out_shape=[jax.ShapeDtypeStruct((rows, columns), F32)] * offsets
        + [jax.ShapeDtypeStruct((2, columns), F32)],
        compiler_params=params(),
        cost_estimate=cost(12 * angles * block * rows * offsets * columns // angles, 8 * MIB),
        name="detector",
    )(ahead, back, gains, measured, *lines, *after)


def scatter_kernel(sums, onehot, out):
    blocks, wide = onehot.shape
    block = wide // 2
    columns = sums.shape[1]
    mine = (
        lax.broadcasted_iota(jnp.int32, (blocks, columns), 1) // block
        == lax.broadcasted_iota(jnp.int32, (blocks, columns), 0)
    )
    cross = jnp.sum(jnp.where(mine, sums[0:1, :], 0.0), axis=1, keepdims=True)
    energy = jnp.sum(jnp.where(mine, sums[1:2, :], 0.0), axis=1, keepdims=True)
    lows = onehot[:, block:]
    value = jnp.concatenate([cross * lows, energy * lows], axis=1)
    first = value.astype(BF16)
    rest = value - first.astype(F32)
    second = rest.astype(BF16)
    third = (rest - second.astype(F32)).astype(BF16)
    highs = onehot[:, :block].astype(BF16).astype(F32).T.astype(BF16)
    out[...] = jnp.dot(
        jnp.concatenate([highs] * 3, axis=1),
        jnp.concatenate([first, second, third], axis=0),
        preferred_element_type=F32,
    )


def scatter(sums, onehot):
    blocks, wide = onehot.shape
    return pl.pallas_call(
        scatter_kernel,
        out_shape=jax.ShapeDtypeStruct((blocks, wide), F32),
        compiler_params=params(),
        cost_estimate=cost(4 * blocks * sums.shape[1], MIB // 8),
        name="scatter",
    )(sums, onehot)


def smooth_kernel(slabs, volume, leading, trailing, *rest):
    out = rest[-1]
    planes, rows, columns = volume.shape
    swap = heading() < 0
    slab = lax.axis_index("slab")
    below = jnp.where(swap, trailing[...], leading[...])
    above = jnp.where(swap, leading[...], trailing[...])
    below = jnp.where(slab == 0, 0.0, below)
    above = jnp.where(slab == slabs - 1, 0.0, above)
    lane = lax.broadcasted_iota(jnp.int32, (rows, columns), 1)
    last = lane == columns - 1
    begin = lane == 0

    def fluxes(here, after):
        ahead = jnp.where(last, 0.0, pltpu.roll(here, columns - 1, 1))
        diff_z = after - here
        diff_u = ahead - here
        scale = lax.rsqrt(diff_z * diff_z + diff_u * diff_u + 0.25)
        return diff_z * scale, diff_u * scale

    flux_below, _ = fluxes(below, volume[0])
    for plane in range(planes):
        here = volume[plane]
        after = volume[plane + 1] if plane + 1 < planes else above
        flux_z, flux_u = fluxes(here, after)
        moved = jnp.where(begin, 0.0, pltpu.roll(flux_u, 1, 1))
        out[plane] = here - 0.2 * (flux_below - flux_z + moved - flux_u)
        flux_below = flux_z


def smooth(volume, leading, trailing, slabs, after):
    planes, depth, columns = volume.shape
    rows = 8
    block = pl.BlockSpec((planes, rows, columns), lambda i: (0, i, 0))
    edge = pl.BlockSpec((rows, columns), lambda i: (i, 0))
    return pl.pallas_call(
        functools.partial(smooth_kernel, slabs),
        grid=(depth // rows,),
        in_specs=[block, edge, edge] + [pl.BlockSpec(memory_space=pl.ANY)] * len(after),
        out_specs=block,
        out_shape=jax.ShapeDtypeStruct(volume.shape, F32),
        compiler_params=params(),
        cost_estimate=cost(40 * planes * depth * columns, 5 * MIB),
        name="smooth",
    )(volume, leading, trailing, *after)


def update_kernel(count, weights, base, *refs):
    images, out, turned = refs[:count], refs[-2], refs[-1]
    planes, depth, width = base.shape

    @pl.when(pl.program_id(0) == 0)
    def _():
        high, low = split(weights[...].T)
        turned[...] = jnp.concatenate([high, low, high], axis=1)

    high, low = split(jnp.concatenate([image[...] for image in images], axis=0))
    gradient = jnp.dot(
        turned[...], jnp.concatenate([high, high, low], axis=0), preferred_element_type=F32
    )
    out[...] = base[...] - 0.2 * gradient.reshape(planes, depth, width)


def update(weights, base, images, after=(), steps=4):
    planes, depth, columns = base.shape
    width = columns // steps
    rows = images[0].shape[0]
    block = pl.BlockSpec((planes, depth, width), lambda i: (0, 0, i))
    return pl.pallas_call(
        functools.partial(update_kernel, len(images)),
        grid=(steps,),
        in_specs=[full(weights.shape), block]
        + [pl.BlockSpec((rows, width), lambda i: (0, i))] * len(images)
        + [pl.BlockSpec(memory_space=pl.ANY)] * len(after),
        out_specs=block,
        out_shape=jax.ShapeDtypeStruct(base.shape, F32),
        scratch_shapes=[pltpu.VMEM((weights.shape[1], 3 * weights.shape[0]), BF16)],
        compiler_params=params(),
        cost_estimate=cost(6 * weights.size * columns, 5 * MIB),
        name="update",
    )(weights, base, *images, *after)


def local(volume, measured, incidence, row_weights, path_table, subset, gain_map, gain_values):
    slabs = lax.axis_size("slab")
    parts = lax.axis_size("ang")
    both = ("slab", "ang")

    def neighbours(turn):
        pairs = []
        for slab in range(slabs):
            for part in range(parts):
                target = slab + 1 - 2 * ((part + turn) % 2)
                if 0 <= target < slabs:
                    pairs.append((slab * parts + part, target * parts + part))
                else:
                    pairs.append((slab * parts + part, slab * parts + (part ^ 1)))
        return pairs

    def flipped(bit):
        return [(i, i ^ bit) for i in range(slabs * parts)]

    def send(value, pairs):
        return lax.ppermute(value, both, pairs)

    first, second = neighbours(0), neighbours(1)
    mates, partners = flipped(1), flipped(2)

    mate_far, mate_near, far, near, weights, leading, trailing = make_lines(
        subset, path_table, volume
    )
    far = send(add(far, send(mate_far, mates)), partners)
    line = add(near, send(mate_near, mates), far)

    line_0 = send(line, first)
    line_1 = send(line, second)
    line_2 = send(line_0, first)
    line_3 = send(line_1, second)

    ahead, back, gains, onehot, leading = prepare(
        incidence, row_weights, gain_map, gain_values, slabs, (line_0, line_1), leading
    )
    leading = send(leading, first)

    *terms, sums = detector(
        ahead, back, gains, measured, (line_0, line_1, line_2, line_3, line)
    )
    to_first = send(terms[3], first)
    to_second = send(terms[2], second)

    totals = scatter(sums, onehot)
    totals = totals + send(totals, mates)

    to_first_next = add(terms[1], to_first, after=(totals,))
    to_second_next, trailing = add(
        terms[0], to_second, after=(totals, leading), through=(trailing,)
    )
    totals = add(totals, send(totals, partners), after=(to_first_next, to_second_next))
    from_first = send(to_first_next, first)
    from_second = send(to_second_next, second)
    trailing = send(trailing, second)

    totals = totals + send(totals, flipped(8 * parts))

    own = add(terms[4], from_first, from_second, after=(totals,))
    mate_own = send(own, mates)
    other = send(own, partners)
    mate_other = send(other, mates)

    base = smooth(volume, leading, trailing, slabs, after=(own,))
    totals = add(totals, send(totals, flipped(16 * parts)), after=(own, base))
    for bit in (32, 1, 2, 4):
        totals = totals + send(totals, flipped(bit * parts))

    volume_next = update(weights, base, (mate_other, mate_own, other, own))

    side = totals.shape[1] // 2
    gain_next = gain_values - (totals[:, :side] / (totals[:, side:] + 1.0)).reshape(-1)
    return volume_next, gain_next


def solution(mesh):
    in_specs = (
        P("slab", "ang", None),
        P("ang", "slab", None),
        P("ang", "slab", None),
        P("ang", None, None, None),
        P(None, "ang"),
        P(),
        P("slab", None),
        P(),
    )
    out_specs = (P("slab", "ang", None), P())
    return jax.shard_map(local, mesh=mesh, in_specs=in_specs, out_specs=out_specs, check_vma=False)
```

```python
import functools

import jax
import jax.numpy as jnp
from jax import lax
from jax.experimental import pallas as pl
from jax.experimental.pallas import tpu as pltpu
from jax.sharding import PartitionSpec as P

F32 = jnp.float32
BF16 = jnp.bfloat16
MIB = 1024 * 1024
LINES_LIMIT = 50


def split(value):
    high = value.astype(BF16)
    low = (value - high.astype(F32)).astype(BF16)
    return high, low


def params(limit=12):
    return pltpu.CompilerParams(vmem_limit_bytes=limit * MIB)


def cost(flops, moved):
    return pl.CostEstimate(flops=flops, bytes_accessed=moved, transcendentals=0)


def full(shape):
    return pl.BlockSpec(shape, lambda i: (0,) * len(shape))


def heading():
    return 1 - 2 * (lax.axis_index("slab") & 1)


def order_of(offsets):
    reach = offsets // 2
    ahead = heading()
    return (reach + ahead, reach - ahead, reach - 2 * ahead, reach + 2 * ahead, reach)


def lines_kernel(steps, subset_in, table_in, volume, *rest):
    outs, weights_out, leading, trailing = rest[:4], rest[4], rest[5], rest[6]
    held, table, subset, sems = rest[7:]
    planes, depth, columns = held.shape
    width = columns // steps
    groups = 4
    angles = weights_out.shape[0] // planes
    each = angles // groups

    def copy(step):
        run = pl.ds(step * width, width)
        return pltpu.make_async_copy(
            volume.at[:, :, run], held.at[:, :, run], sems.at[step]
        )

    subset_copy = pltpu.make_async_copy(subset_in, subset, sems.at[steps])
    table_copy = pltpu.make_async_copy(table_in, table, sems.at[steps + 1])
    subset_copy.start()
    table_copy.start()
    for step in range(steps):
        copy(step).start()

    subset_copy.wait()
    me = lax.axis_index("ang")
    slot = lax.broadcasted_iota(jnp.int32, (angles, 1), 0)
    wanted = jnp.zeros((angles, 1), jnp.int32)
    for group, owner in enumerate((3 - me, me ^ 1, me ^ 2, me)):
        for i in range(each):
            wanted = jnp.where(slot == group * each + i, subset[owner * each + i], wanted)
    entries = table.shape[1]
    onehot = jnp.where(
        lax.broadcasted_iota(jnp.int32, (angles, entries), 1) == wanted, 1.0, 0.0
    ).astype(BF16)
    picked = jnp.zeros((angles, depth), F32)
    table_copy.wait()
    rest_of = table[...]
    for _ in range(3):
        part = rest_of.astype(BF16)
        picked = picked + lax.dot_general(
            onehot, part, (((1,), (1,)), ((), ())), preferred_element_type=F32
        )
        rest_of = rest_of - part.astype(F32)
    wide = jnp.concatenate([picked] * planes, axis=1)
    mask = (
        lax.broadcasted_iota(jnp.int32, (planes, planes * depth), 0)
        == lax.broadcasted_iota(jnp.int32, (planes, planes * depth), 1) // depth
    )
    for angle in range(angles):
        row = jnp.broadcast_to(wide[angle : angle + 1], mask.shape)
        weights_out[angle * planes : (angle + 1) * planes, :] = jnp.where(mask, row, 0.0)
    high_w, low_w = split(weights_out[...])
    both_w = jnp.concatenate([high_w, low_w], axis=0)
    count = angles * planes
    size = count // groups
    first = jnp.where(heading() > 0, planes - 1, 0)
    for step in range(steps):
        copy(step).wait()
        run = slice(step * width, (step + 1) * width)
        leading[:, run] = held[first, :, run]
        trailing[:, run] = held[planes - 1 - first, :, run]
        high, low = split(held[:, :, run].reshape(planes * depth, width))
        main = jnp.dot(both_w, high, preferred_element_type=F32)
        lines = (
            main[:count]
            + main[count:]
            + jnp.dot(high_w, low, preferred_element_type=F32)
        )
        for group in range(groups):
            outs[group][:, run] = lines[group * size : (group + 1) * size]


def make_lines(subset, path_table, volume, steps=4):
    planes, depth, columns = volume.shape
    angles = subset.shape[0]
    rows = angles * planes // 4
    vmem = pl.BlockSpec(memory_space=pltpu.VMEM)
    return pl.pallas_call(
        functools.partial(lines_kernel, steps),
        in_specs=[pl.BlockSpec(memory_space=pl.ANY)] * 3,
        out_specs=[vmem] * 7,
        out_shape=[jax.ShapeDtypeStruct((rows, columns), F32)] * 4
        + [jax.ShapeDtypeStruct((angles * planes, planes * depth), F32)]
        + [jax.ShapeDtypeStruct((depth, columns), F32)] * 2,
        scratch_shapes=[
            pltpu.VMEM((planes, depth, columns), F32),
            pltpu.VMEM(path_table.shape[::-1], F32),
            pltpu.SMEM(subset.shape, jnp.int32),
            pltpu.SemaphoreType.DMA((steps + 2,)),
        ],
        compiler_params=params(LINES_LIMIT),
        cost_estimate=cost(6 * angles * planes * depth * columns, 3 * MIB),
        name="lines",
    )(subset, path_table.T, volume)


def add_kernel(count, *refs):
    total = refs[0][...]
    for ref in refs[1:count]:
        total = total + ref[...]
    out = refs[-1]
    out[...] = total


def add_through_kernel(count, passed, *refs):
    add_kernel(count, *refs[: len(refs) - passed])


def add(*values, after=(), through=()):
    vmem = pl.BlockSpec(memory_space=pltpu.VMEM)
    anywhere = pl.BlockSpec(memory_space=pl.ANY)
    count = len(values) + len(after)
    outs = pl.pallas_call(
        functools.partial(add_through_kernel, len(values), len(through)),
        in_specs=[vmem] * len(values) + [anywhere] * (len(after) + len(through)),
        out_specs=[vmem] + [anywhere] * len(through),
        out_shape=[jax.ShapeDtypeStruct(values[0].shape, F32)]
        + [jax.ShapeDtypeStruct(value.shape, value.dtype) for value in through],
        input_output_aliases={count + i: 1 + i for i in range(len(through))},
        compiler_params=params(8),
        cost_estimate=cost(values[0].size * len(values), values[0].size * 4 * len(values)),
        name="add",
    )(*values, *after, *through)
    return outs if through else outs[0]


def prepare_kernel(slabs, incidence, row_weights, gain_map, gain_values, *rest):
    ahead, back, gains = rest[-6:-3]
    flat = rest[-1]
    angles, offsets, planes, block = row_weights.shape
    flat[...] = jnp.zeros_like(flat)
    slab = lax.axis_index("slab")
    for spot, offset in enumerate(order_of(offsets)):
        other = slab + offset - offsets // 2
        inside = jnp.where((other >= 0) & (other < slabs), 1, 0)
        for angle in range(angles):
            factor = (incidence[angle, 0, offset] * inside).astype(F32)
            at = (spot * angles + angle) * planes
            flat[at : at + planes, angle * block : (angle + 1) * block] = (
                row_weights[angle, offset] * factor
            )
    high, low = split(flat[...])
    back[...] = jnp.concatenate([high, low], axis=0)
    turned = flat[...].T
    high, low = split(turned)
    ahead[...] = jnp.concatenate([high, low, high], axis=1)
    lane = lax.broadcasted_iota(jnp.int32, (1, 2 * block), 1)
    first = lane < block
    blocks = gain_map.shape[1]
    for i in range(blocks // 2):
        low_gain = gain_values[gain_map[0, 2 * i]]
        high_gain = gain_values[gain_map[0, 2 * i + 1]]
        gains[:, 2 * i * block : 2 * (i + 1) * block] = jnp.where(first, low_gain, high_gain)


def prepare(incidence, row_weights, gain_map, gain_values, slabs, after, through):
    angles, offsets, planes, block = row_weights.shape
    rows = offsets * angles * planes
    columns = gain_map.shape[1] * block
    smem = pl.BlockSpec(memory_space=pltpu.SMEM)
    anywhere = pl.BlockSpec(memory_space=pl.ANY)
    vmem = pl.BlockSpec(memory_space=pltpu.VMEM)
    return pl.pallas_call(
        functools.partial(prepare_kernel, slabs),
        in_specs=[smem, vmem, smem, smem] + [anywhere] * (len(after) + len(through)),
        out_specs=[vmem] * 3 + [anywhere] * len(through),
        out_shape=[
            jax.ShapeDtypeStruct((angles * block, 3 * rows), BF16),
            jax.ShapeDtypeStruct((2 * rows, angles * block), BF16),
            jax.ShapeDtypeStruct((1, columns), F32),
        ]
        + [jax.ShapeDtypeStruct(value.shape, F32) for value in through],
        input_output_aliases={4 + len(after) + i: 3 + i for i in range(len(through))},
        scratch_shapes=[pltpu.VMEM((rows, angles * block), F32)],
        compiler_params=params(),
        cost_estimate=cost(1000000, 1 * MIB),
        name="prepare",
    )(incidence, row_weights, gain_map, gain_values, *after, *through)


def detector_kernel(offsets, ahead, back, gains, measured, *refs):
    lines = refs[:offsets]
    outs = refs[-1 - offsets : -1]
    sums = refs[-1]
    angles, block, width = measured.shape
    high, low = split(jnp.concatenate([line[...] for line in lines], axis=0))
    stacked = jnp.concatenate([high, high, low], axis=0)
    forward = jnp.dot(ahead[...], stacked, preferred_element_type=F32)
    gain = gains[...]
    residual = gain * forward - measured[...].reshape(angles * block, width)
    weighted = gain * residual
    cross = jnp.sum(residual * forward, axis=0, keepdims=True)
    energy = jnp.sum(forward * forward, axis=0, keepdims=True)
    sums[...] = jnp.concatenate([cross, energy], axis=0)
    high, low = split(weighted)
    count = back.shape[0] // 2
    main = jnp.dot(back[...], high, preferred_element_type=F32)
    planes = (
        main[:count] + main[count:] + jnp.dot(back[:count], low, preferred_element_type=F32)
    )
    size = count // offsets
    for offset in range(offsets):
        outs[offset][...] = planes[offset * size : (offset + 1) * size]


def detector(ahead, back, gains, measured, lines, after=(), steps=4):
    offsets = len(lines)
    angles, block, columns = measured.shape
    rows = lines[0].shape[0]
    width = columns // steps
    piece = pl.BlockSpec((rows, width), lambda i: (0, i))
    return pl.pallas_call(
        functools.partial(detector_kernel, offsets),
        grid=(steps,),
        in_specs=[
            full(ahead.shape),
            full(back.shape),
            pl.BlockSpec((1, width), lambda i: (0, i)),
            pl.BlockSpec((angles, block, width), lambda i: (0, 0, i)),
        ]
        + [piece] * offsets
        + [pl.BlockSpec(memory_space=pl.ANY)] * len(after),
        out_specs=[piece] * offsets + [pl.BlockSpec((2, width), lambda i: (0, i))],
        out_shape=[jax.ShapeDtypeStruct((rows, columns), F32)] * offsets
        + [jax.ShapeDtypeStruct((2, columns), F32)],
        compiler_params=params(),
        cost_estimate=cost(12 * angles * block * rows * offsets * columns // angles, 8 * MIB),
        name="detector",
    )(ahead, back, gains, measured, *lines, *after)


def group_kernel(blocks, sums, out):
    columns = sums.shape[1]
    block = columns // blocks
    mine = (
        lax.broadcasted_iota(jnp.int32, (blocks, columns), 1) // block
        == lax.broadcasted_iota(jnp.int32, (blocks, columns), 0)
    )
    cross = jnp.sum(jnp.where(mine, sums[0:1, :], 0.0), axis=1, keepdims=True)
    energy = jnp.sum(jnp.where(mine, sums[1:2, :], 0.0), axis=1, keepdims=True)
    row = lax.broadcasted_iota(jnp.int32, (blocks, 2 * blocks), 0)
    lane = lax.broadcasted_iota(jnp.int32, (blocks, 2 * blocks), 1)
    both = jnp.where(lane == row, cross, 0.0) + jnp.where(lane == row + blocks, energy, 0.0)
    out[...] = jnp.sum(both, axis=0, keepdims=True)


def group(sums, blocks):
    return pl.pallas_call(
        functools.partial(group_kernel, blocks),
        out_shape=jax.ShapeDtypeStruct((1, 2 * blocks), F32),
        compiler_params=params(),
        cost_estimate=cost(4 * blocks * sums.shape[1], MIB // 8),
        name="group",
    )(sums)


def spread_kernel(first, second, gain_map, *rest):
    out = rest[-1]
    blocks = gain_map.shape[1]
    index = gain_map[...].astype(F32)
    row = jnp.concatenate([first[...] + second[...], index, index], axis=1)
    out[...] = jnp.broadcast_to(row, out.shape)


def spread(first, second, gain_map, slabs, after):
    vmem = pl.BlockSpec(memory_space=pltpu.VMEM)
    return pl.pallas_call(
        spread_kernel,
        in_specs=[vmem] * 3 + [pl.BlockSpec(memory_space=pl.ANY)] * len(after),
        out_specs=vmem,
        out_shape=jax.ShapeDtypeStruct((slabs, 4 * gain_map.shape[1]), F32),
        compiler_params=params(),
        cost_estimate=cost(slabs * 256, MIB // 8),
        name="spread",
    )(first, second, gain_map, *after)


def gather_kernel(rows, out, highs, values):
    slabs = rows.shape[0]
    side = out.shape[0]
    half = slabs // 2
    whole = rows[...]

    def paired(at):
        part = whole[:, at * side : (at + 1) * side]
        return jnp.concatenate([part[:half], part[half:]], axis=1)

    index = paired(2).astype(jnp.int32)
    high = index // side
    low = index - high * side
    pieces = []
    for value in (paired(0), paired(1)):
        first = value.astype(BF16).astype(F32)
        second = (value - first).astype(BF16).astype(F32)
        pieces.append((first, second, value - first - second))
    place = lax.broadcasted_iota(jnp.int32, (side, 2 * side), 0)
    for p in range(half):
        run = slice(p * 2 * side, (p + 1) * 2 * side)
        highs[:, run] = jnp.where(place == high[p : p + 1], 1.0, 0.0).astype(BF16)
        mask = place == low[p : p + 1]
        for k in range(3):
            for kind in range(2):
                piece = jnp.where(mask, pieces[kind][k][p : p + 1], 0.0)
                values[k, kind * side : (kind + 1) * side, run] = piece.astype(BF16)
    total = jnp.zeros((side, 2 * side), F32)
    for k in range(3):
        total = total + lax.dot_general(
            highs[...], values[k], (((1,), (1,)), ((), ())), preferred_element_type=F32
        )
    out[...] = total[:, :side] / (total[:, side:] + 1.0)


def gather(rows):
    slabs = rows.shape[0]
    side = rows.shape[1] // 4
    return pl.pallas_call(
        gather_kernel,
        out_shape=jax.ShapeDtypeStruct((side, side), F32),
        scratch_shapes=[
            pltpu.VMEM((side, slabs * side), BF16),
            pltpu.VMEM((3, 2 * side, slabs * side), BF16),
        ],
        compiler_params=params(),
        cost_estimate=cost(6 * side * side * 2 * slabs * side, MIB),
        name="gather",
    )(rows)


def hand_kernel(*refs):
    del refs


def hand(value, after):
    anywhere = pl.BlockSpec(memory_space=pl.ANY)
    return pl.pallas_call(
        hand_kernel,
        in_specs=[anywhere] * 2,
        out_specs=anywhere,
        out_shape=jax.ShapeDtypeStruct(value.shape, value.dtype),
        input_output_aliases={0: 0},
        compiler_params=params(),
        cost_estimate=cost(0, 0),
        name="hand",
    )(value, after)


def smooth_kernel(slabs, volume, leading, trailing, *rest):
    out = rest[-1]
    planes, rows, columns = volume.shape
    swap = heading() > 0
    slab = lax.axis_index("slab")
    below = jnp.where(swap, trailing[...], leading[...])
    above = jnp.where(swap, leading[...], trailing[...])
    below = jnp.where(slab == 0, 0.0, below)
    above = jnp.where(slab == slabs - 1, 0.0, above)
    lane = lax.broadcasted_iota(jnp.int32, (rows, columns), 1)
    last = lane == columns - 1
    begin = lane == 0

    def fluxes(here, after):
        ahead = jnp.where(last, 0.0, pltpu.roll(here, columns - 1, 1))
        diff_z = after - here
        diff_u = ahead - here
        scale = lax.rsqrt(diff_z * diff_z + diff_u * diff_u + 0.25)
        return diff_z * scale, diff_u * scale

    flux_below, _ = fluxes(below, volume[0])
    for plane in range(planes):
        here = volume[plane]
        after = volume[plane + 1] if plane + 1 < planes else above
        flux_z, flux_u = fluxes(here, after)
        moved = jnp.where(begin, 0.0, pltpu.roll(flux_u, 1, 1))
        out[plane] = here - 0.2 * (flux_below - flux_z + moved - flux_u)
        flux_below = flux_z


def smooth(volume, leading, trailing, slabs, after):
    planes, depth, columns = volume.shape
    rows = 8
    block = pl.BlockSpec((planes, rows, columns), lambda i: (0, i, 0))
    edge = pl.BlockSpec((rows, columns), lambda i: (i, 0))
    return pl.pallas_call(
        functools.partial(smooth_kernel, slabs),
        grid=(depth // rows,),
        in_specs=[block, edge, edge] + [pl.BlockSpec(memory_space=pl.ANY)] * len(after),
        out_specs=block,
        out_shape=jax.ShapeDtypeStruct(volume.shape, F32),
        compiler_params=params(),
        cost_estimate=cost(40 * planes * depth * columns, 5 * MIB),
        name="smooth",
    )(volume, leading, trailing, *after)


def update_kernel(count, weights, base, *refs):
    images, out, turned = refs[:count], refs[-2], refs[-1]
    planes, depth, width = base.shape

    @pl.when(pl.program_id(0) == 0)
    def _():
        high, low = split(weights[...].T)
        turned[...] = jnp.concatenate([high, low, high], axis=1)

    high, low = split(jnp.concatenate([image[...] for image in images], axis=0))
    gradient = jnp.dot(
        turned[...], jnp.concatenate([high, high, low], axis=0), preferred_element_type=F32
    )
    out[...] = base[...] - 0.2 * gradient.reshape(planes, depth, width)


def update(weights, base, images, after=(), steps=4):
    planes, depth, columns = base.shape
    width = columns // steps
    rows = images[0].shape[0]
    block = pl.BlockSpec((planes, depth, width), lambda i: (0, 0, i))
    return pl.pallas_call(
        functools.partial(update_kernel, len(images)),
        grid=(steps,),
        in_specs=[full(weights.shape), block]
        + [pl.BlockSpec((rows, width), lambda i: (0, i))] * len(images)
        + [pl.BlockSpec(memory_space=pl.ANY)] * len(after),
        out_specs=block,
        out_shape=jax.ShapeDtypeStruct(base.shape, F32),
        scratch_shapes=[pltpu.VMEM((weights.shape[1], 3 * weights.shape[0]), BF16)],
        compiler_params=params(),
        cost_estimate=cost(6 * weights.size * columns, 5 * MIB),
        name="update",
    )(weights, base, *images, *after)


def local(volume, measured, incidence, row_weights, path_table, subset, gain_map, gain_values):
    slabs = lax.axis_size("slab")
    parts = lax.axis_size("ang")
    both = ("slab", "ang")

    def neighbours(turn):
        pairs = []
        for slab in range(slabs):
            for part in range(parts):
                target = slab + 1 - 2 * ((slab + turn) % 2)
                if 0 <= target < slabs:
                    pairs.append((slab * parts + part, target * parts + part))
                else:
                    pairs.append((slab * parts + part, slab * parts + (part ^ 1)))
        return pairs

    def flipped(bit):
        return [(i, i ^ bit) for i in range(slabs * parts)]

    def send(value, pairs):
        return lax.ppermute(value, both, pairs)

    first, second = neighbours(0), neighbours(1)
    mates, partners = flipped(1), flipped(2)

    mate_far, mate_near, far, near, weights, leading, trailing = make_lines(
        subset, path_table, volume
    )
    far = send(add(far, send(mate_far, mates)), partners)
    line = add(near, send(mate_near, mates), far)

    line_0 = send(line, first)
    line_1 = send(line, second)
    line_2 = send(line_0, second)
    line_3 = send(line_1, first)

    ahead, back, gains, leading, trailing = prepare(
        incidence,
        row_weights,
        gain_map,
        gain_values,
        slabs,
        (line_0, line_1),
        (leading, trailing),
    )
    leading = send(leading, first)
    trailing = send(trailing, second)

    *terms, sums = detector(
        ahead, back, gains, measured, (line_0, line_1, line_2, line_3, line)
    )
    to_first = send(terms[3], first)
    to_second = send(terms[2], second)

    totals = group(sums, gain_map.shape[1])
    totals = totals + send(totals, mates)
    base = smooth(volume, leading, trailing, slabs, after=(totals,))

    to_second_next = add(terms[1], to_first, after=(base,))
    to_first_next = add(terms[0], to_second, after=(base,))
    other_totals = send(totals, partners)
    from_second = send(to_second_next, second)
    from_first = send(to_first_next, first)

    own = add(terms[4], from_first, from_second, after=(other_totals,))
    mate_own = send(own, mates)
    other = send(own, partners)

    rows = spread(totals, other_totals, gain_map, slabs, after=(mate_own,))
    rows = lax.all_to_all(rows, "slab", split_axis=0, concat_axis=0, tiled=True)
    other = hand(other, rows)
    mate_other = send(other, mates)
    gain_next = gain_values - gather(rows).reshape(-1)

    volume_next = update(weights, base, (mate_other, mate_own, other, own))
    return volume_next, gain_next


def solution(mesh):
    in_specs = (
        P("slab", "ang", None),
        P("ang", "slab", None),
        P("ang", "slab", None),
        P("ang", None, None, None),
        P(None, "ang"),
        P(),
        P("slab", None),
        P(),
    )
    out_specs = (P("slab", "ang", None), P())
    return jax.shard_map(local, mesh=mesh, in_specs=in_specs, out_specs=out_specs, check_vma=False)
```

```python
import functools

import jax
import jax.numpy as jnp
from jax import lax
from jax.experimental import pallas as pl
from jax.experimental.pallas import tpu as pltpu
from jax.sharding import PartitionSpec as P

F32 = jnp.float32
BF16 = jnp.bfloat16
MIB = 1024 * 1024
LINES_LIMIT = 50


def split(value):
    high = value.astype(BF16)
    low = (value - high.astype(F32)).astype(BF16)
    return high, low


def params(limit=12):
    return pltpu.CompilerParams(vmem_limit_bytes=limit * MIB)


def cost(flops, moved):
    return pl.CostEstimate(flops=flops, bytes_accessed=moved, transcendentals=0)


def full(shape):
    return pl.BlockSpec(shape, lambda i: (0,) * len(shape))


def heading():
    return 1 - 2 * (lax.axis_index("slab") & 1)


def order_of(offsets):
    reach = offsets // 2
    ahead = heading()
    return (reach + ahead, reach - ahead, reach - 2 * ahead, reach + 2 * ahead, reach)


def lines_kernel(steps, subset_in, table_in, volume, *rest):
    outs, weights_out, leading, trailing = rest[:4], rest[4], rest[5], rest[6]
    held, table, subset, sems = rest[7:]
    planes, depth, columns = held.shape
    width = columns // steps
    groups = 4
    angles = weights_out.shape[0] // planes
    each = angles // groups

    def copy(step):
        run = pl.ds(step * width, width)
        return pltpu.make_async_copy(
            volume.at[:, :, run], held.at[:, :, run], sems.at[step]
        )

    subset_copy = pltpu.make_async_copy(subset_in, subset, sems.at[steps])
    table_copy = pltpu.make_async_copy(table_in, table, sems.at[steps + 1])
    subset_copy.start()
    table_copy.start()
    for step in range(steps):
        copy(step).start()

    subset_copy.wait()
    me = lax.axis_index("ang")
    slot = lax.broadcasted_iota(jnp.int32, (angles, 1), 0)
    wanted = jnp.zeros((angles, 1), jnp.int32)
    for group, owner in enumerate((3 - me, me ^ 1, me ^ 2, me)):
        for i in range(each):
            wanted = jnp.where(slot == group * each + i, subset[owner * each + i], wanted)
    entries = table.shape[1]
    onehot = jnp.where(
        lax.broadcasted_iota(jnp.int32, (angles, entries), 1) == wanted, 1.0, 0.0
    ).astype(BF16)
    picked = jnp.zeros((angles, depth), F32)
    table_copy.wait()
    rest_of = table[...]
    for _ in range(3):
        part = rest_of.astype(BF16)
        picked = picked + lax.dot_general(
            onehot, part, (((1,), (1,)), ((), ())), preferred_element_type=F32
        )
        rest_of = rest_of - part.astype(F32)
    wide = jnp.concatenate([picked] * planes, axis=1)
    mask = (
        lax.broadcasted_iota(jnp.int32, (planes, planes * depth), 0)
        == lax.broadcasted_iota(jnp.int32, (planes, planes * depth), 1) // depth
    )
    for angle in range(angles):
        row = jnp.broadcast_to(wide[angle : angle + 1], mask.shape)
        weights_out[angle * planes : (angle + 1) * planes, :] = jnp.where(mask, row, 0.0)
    high_w, low_w = split(weights_out[...])
    both_w = jnp.concatenate([high_w, low_w], axis=0)
    count = angles * planes
    size = count // groups
    first = jnp.where(heading() > 0, planes - 1, 0)
    for step in range(steps):
        copy(step).wait()
        run = slice(step * width, (step + 1) * width)
        leading[:, run] = held[first, :, run]
        trailing[:, run] = held[planes - 1 - first, :, run]
        high, low = split(held[:, :, run].reshape(planes * depth, width))
        main = jnp.dot(both_w, high, preferred_element_type=F32)
        lines = (
            main[:count]
            + main[count:]
            + jnp.dot(high_w, low, preferred_element_type=F32)
        )
        for group in range(groups):
            outs[group][:, run] = lines[group * size : (group + 1) * size]


def make_lines(subset, path_table, volume, steps=4):
    planes, depth, columns = volume.shape
    angles = subset.shape[0]
    rows = angles * planes // 4
    vmem = pl.BlockSpec(memory_space=pltpu.VMEM)
    return pl.pallas_call(
        functools.partial(lines_kernel, steps),
        in_specs=[pl.BlockSpec(memory_space=pl.ANY)] * 3,
        out_specs=[vmem] * 7,
        out_shape=[jax.ShapeDtypeStruct((rows, columns), F32)] * 4
        + [jax.ShapeDtypeStruct((angles * planes, planes * depth), F32)]
        + [jax.ShapeDtypeStruct((depth, columns), F32)] * 2,
        scratch_shapes=[
            pltpu.VMEM((planes, depth, columns), F32),
            pltpu.VMEM(path_table.shape[::-1], F32),
            pltpu.SMEM(subset.shape, jnp.int32),
            pltpu.SemaphoreType.DMA((steps + 2,)),
        ],
        compiler_params=params(LINES_LIMIT),
        cost_estimate=cost(6 * angles * planes * depth * columns, 3 * MIB),
        name="lines",
    )(subset, path_table.T, volume)


def add_kernel(count, *refs):
    total = refs[0][...]
    for ref in refs[1:count]:
        total = total + ref[...]
    out = refs[-1]
    out[...] = total


def add_through_kernel(count, passed, *refs):
    add_kernel(count, *refs[: len(refs) - passed])


def add(*values, after=(), through=()):
    vmem = pl.BlockSpec(memory_space=pltpu.VMEM)
    anywhere = pl.BlockSpec(memory_space=pl.ANY)
    count = len(values) + len(after)
    outs = pl.pallas_call(
        functools.partial(add_through_kernel, len(values), len(through)),
        in_specs=[vmem] * len(values) + [anywhere] * (len(after) + len(through)),
        out_specs=[vmem] + [anywhere] * len(through),
        out_shape=[jax.ShapeDtypeStruct(values[0].shape, F32)]
        + [jax.ShapeDtypeStruct(value.shape, value.dtype) for value in through],
        input_output_aliases={count + i: 1 + i for i in range(len(through))},
        compiler_params=params(8),
        cost_estimate=cost(values[0].size * len(values), values[0].size * 4 * len(values)),
        name="add",
    )(*values, *after, *through)
    return outs if through else outs[0]


def prepare_kernel(slabs, incidence, row_weights, gain_map, gain_values, *rest):
    ahead, back, gains = rest[-6:-3]
    flat = rest[-1]
    angles, offsets, planes, block = row_weights.shape
    flat[...] = jnp.zeros_like(flat)
    slab = lax.axis_index("slab")
    for spot, offset in enumerate(order_of(offsets)):
        other = slab + offset - offsets // 2
        inside = jnp.where((other >= 0) & (other < slabs), 1, 0)
        for angle in range(angles):
            factor = (incidence[angle, 0, offset] * inside).astype(F32)
            at = (spot * angles + angle) * planes
            flat[at : at + planes, angle * block : (angle + 1) * block] = (
                row_weights[angle, offset] * factor
            )
    high, low = split(flat[...])
    back[...] = jnp.concatenate([high, low], axis=0)
    turned = flat[...].T
    high, low = split(turned)
    ahead[...] = jnp.concatenate([high, low, high], axis=1)
    lane = lax.broadcasted_iota(jnp.int32, (1, 2 * block), 1)
    first = lane < block
    blocks = gain_map.shape[1]
    for i in range(blocks // 2):
        low_gain = gain_values[gain_map[0, 2 * i]]
        high_gain = gain_values[gain_map[0, 2 * i + 1]]
        gains[:, 2 * i * block : 2 * (i + 1) * block] = jnp.where(first, low_gain, high_gain)


def prepare(incidence, row_weights, gain_map, gain_values, slabs, after, through):
    angles, offsets, planes, block = row_weights.shape
    rows = offsets * angles * planes
    columns = gain_map.shape[1] * block
    smem = pl.BlockSpec(memory_space=pltpu.SMEM)
    anywhere = pl.BlockSpec(memory_space=pl.ANY)
    vmem = pl.BlockSpec(memory_space=pltpu.VMEM)
    return pl.pallas_call(
        functools.partial(prepare_kernel, slabs),
        in_specs=[smem, vmem, smem, smem] + [anywhere] * (len(after) + len(through)),
        out_specs=[vmem] * 3 + [anywhere] * len(through),
        out_shape=[
            jax.ShapeDtypeStruct((angles * block, 3 * rows), BF16),
            jax.ShapeDtypeStruct((2 * rows, angles * block), BF16),
            jax.ShapeDtypeStruct((1, columns), F32),
        ]
        + [jax.ShapeDtypeStruct(value.shape, F32) for value in through],
        input_output_aliases={4 + len(after) + i: 3 + i for i in range(len(through))},
        scratch_shapes=[pltpu.VMEM((rows, angles * block), F32)],
        compiler_params=params(),
        cost_estimate=cost(1000000, 1 * MIB),
        name="prepare",
    )(incidence, row_weights, gain_map, gain_values, *after, *through)


def detector_kernel(offsets, ahead, back, gains, measured, *refs):
    lines = refs[:offsets]
    outs = refs[-1 - offsets : -1]
    sums = refs[-1]
    angles, block, width = measured.shape
    high, low = split(jnp.concatenate([line[...] for line in lines], axis=0))
    stacked = jnp.concatenate([high, high, low], axis=0)
    forward = jnp.dot(ahead[...], stacked, preferred_element_type=F32)
    gain = gains[...]
    residual = gain * forward - measured[...].reshape(angles * block, width)
    weighted = gain * residual
    cross = jnp.sum(residual * forward, axis=0, keepdims=True)
    energy = jnp.sum(forward * forward, axis=0, keepdims=True)
    sums[...] = jnp.concatenate([cross, energy], axis=0)
    high, low = split(weighted)
    count = back.shape[0] // 2
    main = jnp.dot(back[...], high, preferred_element_type=F32)
    planes = (
        main[:count] + main[count:] + jnp.dot(back[:count], low, preferred_element_type=F32)
    )
    size = count // offsets
    for offset in range(offsets):
        outs[offset][...] = planes[offset * size : (offset + 1) * size]


def detector(ahead, back, gains, measured, lines, after=(), steps=4):
    offsets = len(lines)
    angles, block, columns = measured.shape
    rows = lines[0].shape[0]
    width = columns // steps
    piece = pl.BlockSpec((rows, width), lambda i: (0, i))
    return pl.pallas_call(
        functools.partial(detector_kernel, offsets),
        grid=(steps,),
        in_specs=[
            full(ahead.shape),
            full(back.shape),
            pl.BlockSpec((1, width), lambda i: (0, i)),
            pl.BlockSpec((angles, block, width), lambda i: (0, 0, i)),
        ]
        + [piece] * offsets
        + [pl.BlockSpec(memory_space=pl.ANY)] * len(after),
        out_specs=[piece] * offsets + [pl.BlockSpec((2, width), lambda i: (0, i))],
        out_shape=[jax.ShapeDtypeStruct((rows, columns), F32)] * offsets
        + [jax.ShapeDtypeStruct((2, columns), F32)],
        compiler_params=params(),
        cost_estimate=cost(12 * angles * block * rows * offsets * columns // angles, 8 * MIB),
        name="detector",
    )(ahead, back, gains, measured, *lines, *after)


def group_kernel(blocks, sums, out):
    columns = sums.shape[1]
    block = columns // blocks
    mine = (
        lax.broadcasted_iota(jnp.int32, (blocks, columns), 1) // block
        == lax.broadcasted_iota(jnp.int32, (blocks, columns), 0)
    )
    cross = jnp.sum(jnp.where(mine, sums[0:1, :], 0.0), axis=1, keepdims=True)
    energy = jnp.sum(jnp.where(mine, sums[1:2, :], 0.0), axis=1, keepdims=True)
    row = lax.broadcasted_iota(jnp.int32, (blocks, 2 * blocks), 0)
    lane = lax.broadcasted_iota(jnp.int32, (blocks, 2 * blocks), 1)
    both = jnp.where(lane == row, cross, 0.0) + jnp.where(lane == row + blocks, energy, 0.0)
    out[...] = jnp.sum(both, axis=0, keepdims=True)


def group(sums, blocks):
    return pl.pallas_call(
        functools.partial(group_kernel, blocks),
        out_shape=jax.ShapeDtypeStruct((1, 2 * blocks), F32),
        compiler_params=params(),
        cost_estimate=cost(4 * blocks * sums.shape[1], MIB // 8),
        name="group",
    )(sums)


def spread_kernel(first, second, gain_map, *rest):
    out = rest[-1]
    blocks = gain_map.shape[1]
    index = gain_map[...].astype(F32)
    row = jnp.concatenate([first[...] + second[...], index, index], axis=1)
    out[...] = jnp.broadcast_to(row, out.shape)


def spread(first, second, gain_map, slabs, after):
    vmem = pl.BlockSpec(memory_space=pltpu.VMEM)
    return pl.pallas_call(
        spread_kernel,
        in_specs=[vmem] * 3 + [pl.BlockSpec(memory_space=pl.ANY)] * len(after),
        out_specs=vmem,
        out_shape=jax.ShapeDtypeStruct((slabs, 4 * gain_map.shape[1]), F32),
        compiler_params=params(),
        cost_estimate=cost(slabs * 256, MIB // 8),
        name="spread",
    )(first, second, gain_map, *after)


def gather_kernel(rows, gains, out, values, onehot):
    slabs = rows.shape[0]
    side = rows.shape[1] // 4
    height, width = out.shape
    half = slabs // 2
    whole = rows[...]

    def paired(at):
        part = whole[:, at * side : (at + 1) * side]
        return jnp.concatenate([part[:half], part[half:]], axis=1)

    index = paired(2).astype(jnp.int32)
    high = index // width
    low = index - high * width
    pieces = []
    for value in (paired(0), paired(1)):
        first = value.astype(BF16).astype(F32)
        second = (value - first).astype(BF16).astype(F32)
        pieces.append((first, second, value - first - second))
    row = lax.broadcasted_iota(jnp.int32, (height, 2 * side), 0)
    lane = lax.broadcasted_iota(jnp.int32, (width, 2 * side), 0)
    for p in range(half):
        run = slice(p * 2 * side, (p + 1) * 2 * side)
        onehot[:, run] = jnp.where(lane == low[p : p + 1], 1.0, 0.0).astype(BF16)
        mask = row == high[p : p + 1]
        for k in range(3):
            for kind in range(2):
                at = (2 * k + kind) * height
                piece = jnp.where(mask, pieces[kind][k][p : p + 1], 0.0)
                values[at : at + height, run] = piece.astype(BF16)
    parts = lax.dot_general(
        values[...], onehot[...], (((1,), (1,)), ((), ())), preferred_element_type=F32
    )
    total = parts[: 2 * height] + parts[2 * height : 4 * height] + parts[4 * height :]
    out[...] = gains[...] - total[:height] / (total[height:] + 1.0)


def gather(rows, gain_values):
    slabs = rows.shape[0]
    side = rows.shape[1] // 4
    width = 128
    height = gain_values.shape[0] // width
    return pl.pallas_call(
        gather_kernel,
        out_shape=jax.ShapeDtypeStruct((height, width), F32),
        scratch_shapes=[
            pltpu.VMEM((6 * height, slabs * side), BF16),
            pltpu.VMEM((width, slabs * side), BF16),
        ],
        compiler_params=params(),
        cost_estimate=cost(12 * height * width * slabs * side, MIB),
        name="gather",
    )(rows, gain_values.reshape(height, width)).reshape(-1)


def hand_kernel(*refs):
    del refs


def hand(value, after):
    anywhere = pl.BlockSpec(memory_space=pl.ANY)
    return pl.pallas_call(
        hand_kernel,
        in_specs=[anywhere] * 2,
        out_specs=anywhere,
        out_shape=jax.ShapeDtypeStruct(value.shape, value.dtype),
        input_output_aliases={0: 0},
        compiler_params=params(),
        cost_estimate=cost(0, 0),
        name="hand",
    )(value, after)


def smooth_kernel(slabs, volume, leading, trailing, *rest):
    out = rest[-1]
    planes, rows, columns = volume.shape
    swap = heading() > 0
    slab = lax.axis_index("slab")
    below = jnp.where(swap, trailing[...], leading[...])
    above = jnp.where(swap, leading[...], trailing[...])
    below = jnp.where(slab == 0, 0.0, below)
    above = jnp.where(slab == slabs - 1, 0.0, above)
    lane = lax.broadcasted_iota(jnp.int32, (rows, columns), 1)
    last = lane == columns - 1
    begin = lane == 0

    def fluxes(here, after):
        ahead = jnp.where(last, 0.0, pltpu.roll(here, columns - 1, 1))
        diff_z = after - here
        diff_u = ahead - here
        scale = lax.rsqrt(diff_z * diff_z + diff_u * diff_u + 0.25)
        return diff_z * scale, diff_u * scale

    flux_below, _ = fluxes(below, volume[0])
    for plane in range(planes):
        here = volume[plane]
        after = volume[plane + 1] if plane + 1 < planes else above
        flux_z, flux_u = fluxes(here, after)
        moved = jnp.where(begin, 0.0, pltpu.roll(flux_u, 1, 1))
        out[plane] = here - 0.2 * (flux_below - flux_z + moved - flux_u)
        flux_below = flux_z


def smooth(volume, leading, trailing, slabs, after):
    planes, depth, columns = volume.shape
    rows = 8
    block = pl.BlockSpec((planes, rows, columns), lambda i: (0, i, 0))
    edge = pl.BlockSpec((rows, columns), lambda i: (i, 0))
    return pl.pallas_call(
        functools.partial(smooth_kernel, slabs),
        grid=(depth // rows,),
        in_specs=[block, edge, edge] + [pl.BlockSpec(memory_space=pl.ANY)] * len(after),
        out_specs=block,
        out_shape=jax.ShapeDtypeStruct(volume.shape, F32),
        compiler_params=params(),
        cost_estimate=cost(40 * planes * depth * columns, 5 * MIB),
        name="smooth",
    )(volume, leading, trailing, *after)


def update_kernel(count, weights, base, *refs):
    images, out, turned = refs[:count], refs[-2], refs[-1]
    planes, depth, width = base.shape

    @pl.when(pl.program_id(0) == 0)
    def _():
        high, low = split(weights[...].T)
        turned[...] = jnp.concatenate([high, low, high], axis=1)

    high, low = split(jnp.concatenate([image[...] for image in images], axis=0))
    gradient = jnp.dot(
        turned[...], jnp.concatenate([high, high, low], axis=0), preferred_element_type=F32
    )
    out[...] = base[...] - 0.2 * gradient.reshape(planes, depth, width)


def update(weights, base, images, after=(), steps=4):
    planes, depth, columns = base.shape
    width = columns // steps
    rows = images[0].shape[0]
    block = pl.BlockSpec((planes, depth, width), lambda i: (0, 0, i))
    return pl.pallas_call(
        functools.partial(update_kernel, len(images)),
        grid=(steps,),
        in_specs=[full(weights.shape), block]
        + [pl.BlockSpec((rows, width), lambda i: (0, i))] * len(images)
        + [pl.BlockSpec(memory_space=pl.ANY)] * len(after),
        out_specs=block,
        out_shape=jax.ShapeDtypeStruct(base.shape, F32),
        scratch_shapes=[pltpu.VMEM((weights.shape[1], 3 * weights.shape[0]), BF16)],
        compiler_params=params(),
        cost_estimate=cost(6 * weights.size * columns, 5 * MIB),
        name="update",
    )(weights, base, *images, *after)


def local(volume, measured, incidence, row_weights, path_table, subset, gain_map, gain_values):
    slabs = lax.axis_size("slab")
    parts = lax.axis_size("ang")
    both = ("slab", "ang")

    def neighbours(turn):
        pairs = []
        for slab in range(slabs):
            for part in range(parts):
                target = slab + 1 - 2 * ((slab + turn) % 2)
                if 0 <= target < slabs:
                    pairs.append((slab * parts + part, target * parts + part))
                else:
                    pairs.append((slab * parts + part, slab * parts + (part ^ 1)))
        return pairs

    def flipped(bit):
        return [(i, i ^ bit) for i in range(slabs * parts)]

    def send(value, pairs):
        return lax.ppermute(value, both, pairs)

    first, second = neighbours(0), neighbours(1)
    mates, partners = flipped(1), flipped(2)

    mate_far, mate_near, far, near, weights, leading, trailing = make_lines(
        subset, path_table, volume
    )
    far = send(add(far, send(mate_far, mates)), partners)
    line = add(near, send(mate_near, mates), far)

    line_0 = send(line, first)
    line_1 = send(line, second)
    line_2 = send(line_0, second)
    line_3 = send(line_1, first)

    ahead, back, gains, leading, trailing = prepare(
        incidence,
        row_weights,
        gain_map,
        gain_values,
        slabs,
        (line_0, line_1),
        (leading, trailing),
    )
    leading = send(leading, first)
    trailing = send(trailing, second)

    *terms, sums = detector(
        ahead, back, gains, measured, (line_0, line_1, line_2, line_3, line)
    )
    to_first = send(terms[3], first)
    to_second = send(terms[2], second)

    totals = group(sums, gain_map.shape[1])
    totals = totals + send(totals, mates)
    to_second_next = add(terms[1], to_first, after=(totals,))
    to_first_next = add(terms[0], to_second, after=(totals,))
    other_totals = send(totals, partners)
    from_second = send(to_second_next, second)
    from_first = send(to_first_next, first)

    base = smooth(volume, leading, trailing, slabs, after=(to_first_next, to_second_next))
    own = add(terms[4], from_first, from_second, after=(other_totals, base))
    mate_own = send(own, mates)
    other = send(own, partners)

    rows = spread(totals, other_totals, gain_map, slabs, after=(mate_own,))
    rows = lax.all_to_all(rows, "slab", split_axis=0, concat_axis=0, tiled=True)
    other = hand(other, rows)
    mate_other = send(other, mates)
    gain_next = gather(rows, gain_values)

    volume_next = update(weights, base, (mate_other, mate_own, other, own))
    return volume_next, gain_next


def solution(mesh):
    in_specs = (
        P("slab", "ang", None),
        P("ang", "slab", None),
        P("ang", "slab", None),
        P("ang", None, None, None),
        P(None, "ang"),
        P(),
        P("slab", None),
        P(),
    )
    out_specs = (P("slab", "ang", None), P())
    return jax.shard_map(local, mesh=mesh, in_specs=in_specs, out_specs=out_specs, check_vma=False)
```

```python
import functools

import jax
import jax.numpy as jnp
from jax import lax
from jax.experimental import pallas as pl
from jax.experimental.pallas import tpu as pltpu
from jax.sharding import PartitionSpec as P

F32 = jnp.float32
BF16 = jnp.bfloat16
MIB = 1024 * 1024
LINES_LIMIT = 50


def split(value):
    high = value.astype(BF16)
    low = (value - high.astype(F32)).astype(BF16)
    return high, low


def params(limit=20):
    return pltpu.CompilerParams(vmem_limit_bytes=limit * MIB)


def cost(flops, moved):
    return pl.CostEstimate(flops=flops, bytes_accessed=moved, transcendentals=0)


def full(shape):
    return pl.BlockSpec(shape, lambda i: (0,) * len(shape))


def heading():
    return 1 - 2 * (lax.axis_index("slab") & 1)


def order_of(offsets):
    reach = offsets // 2
    ahead = heading()
    return (reach + ahead, reach - ahead, reach - 2 * ahead, reach + 2 * ahead, reach)


def lines_kernel(steps, subset_in, table_in, volume, *rest):
    outs, weights_out, leading, trailing = rest[:4], rest[4], rest[5], rest[6]
    held, table, subset, sems = rest[7:]
    planes, depth, columns = held.shape
    width = columns // steps
    groups = 4
    angles = weights_out.shape[0] // planes
    each = angles // groups

    def copy(step):
        run = pl.ds(step * width, width)
        return pltpu.make_async_copy(
            volume.at[:, :, run], held.at[:, :, run], sems.at[step]
        )

    subset_copy = pltpu.make_async_copy(subset_in, subset, sems.at[steps])
    table_copy = pltpu.make_async_copy(table_in, table, sems.at[steps + 1])
    subset_copy.start()
    table_copy.start()
    for step in range(steps):
        copy(step).start()

    subset_copy.wait()
    me = lax.axis_index("ang")
    slot = lax.broadcasted_iota(jnp.int32, (angles, 1), 0)
    wanted = jnp.zeros((angles, 1), jnp.int32)
    for group, owner in enumerate((3 - me, me ^ 1, me ^ 2, me)):
        for i in range(each):
            wanted = jnp.where(slot == group * each + i, subset[owner * each + i], wanted)
    entries = table.shape[1]
    onehot = jnp.where(
        lax.broadcasted_iota(jnp.int32, (angles, entries), 1) == wanted, 1.0, 0.0
    ).astype(BF16)
    picked = jnp.zeros((angles, depth), F32)
    table_copy.wait()
    rest_of = table[...]
    for _ in range(3):
        part = rest_of.astype(BF16)
        picked = picked + lax.dot_general(
            onehot, part, (((1,), (1,)), ((), ())), preferred_element_type=F32
        )
        rest_of = rest_of - part.astype(F32)
    wide = jnp.concatenate([picked] * planes, axis=1)
    mask = (
        lax.broadcasted_iota(jnp.int32, (planes, planes * depth), 0)
        == lax.broadcasted_iota(jnp.int32, (planes, planes * depth), 1) // depth
    )
    for angle in range(angles):
        row = jnp.broadcast_to(wide[angle : angle + 1], mask.shape)
        weights_out[angle * planes : (angle + 1) * planes, :] = jnp.where(mask, row, 0.0)
    high_w, low_w = split(weights_out[...])
    both_w = jnp.concatenate([high_w, low_w], axis=0)
    count = angles * planes
    size = count // groups
    first = jnp.where(heading() > 0, planes - 1, 0)
    for step in range(steps):
        copy(step).wait()
        run = slice(step * width, (step + 1) * width)
        leading[:, run] = held[first, :, run]
        trailing[:, run] = held[planes - 1 - first, :, run]
        high, low = split(held[:, :, run].reshape(planes * depth, width))
        main = jnp.dot(both_w, high, preferred_element_type=F32)
        lines = (
            main[:count]
            + main[count:]
            + jnp.dot(high_w, low, preferred_element_type=F32)
        )
        for group in range(groups):
            outs[group][:, run] = lines[group * size : (group + 1) * size]


def make_lines(subset, path_table, volume, steps=4):
    planes, depth, columns = volume.shape
    angles = subset.shape[0]
    rows = angles * planes // 4
    vmem = pl.BlockSpec(memory_space=pltpu.VMEM)
    return pl.pallas_call(
        functools.partial(lines_kernel, steps),
        in_specs=[pl.BlockSpec(memory_space=pl.ANY)] * 3,
        out_specs=[vmem] * 7,
        out_shape=[jax.ShapeDtypeStruct((rows, columns), F32)] * 4
        + [jax.ShapeDtypeStruct((angles * planes, planes * depth), F32)]
        + [jax.ShapeDtypeStruct((depth, columns), F32)] * 2,
        scratch_shapes=[
            pltpu.VMEM((planes, depth, columns), F32),
            pltpu.VMEM(path_table.shape[::-1], F32),
            pltpu.SMEM(subset.shape, jnp.int32),
            pltpu.SemaphoreType.DMA((steps + 2,)),
        ],
        compiler_params=params(LINES_LIMIT),
        cost_estimate=cost(6 * angles * planes * depth * columns, 3 * MIB),
        name="lines",
    )(subset, path_table.T, volume)


def add_kernel(count, *refs):
    total = refs[0][...]
    for ref in refs[1:count]:
        total = total + ref[...]
    out = refs[-1]
    out[...] = total


def add_through_kernel(count, passed, *refs):
    add_kernel(count, *refs[: len(refs) - passed])


def add(*values, after=(), through=()):
    vmem = pl.BlockSpec(memory_space=pltpu.VMEM)
    anywhere = pl.BlockSpec(memory_space=pl.ANY)
    count = len(values) + len(after)
    outs = pl.pallas_call(
        functools.partial(add_through_kernel, len(values), len(through)),
        in_specs=[vmem] * len(values) + [anywhere] * (len(after) + len(through)),
        out_specs=[vmem] + [anywhere] * len(through),
        out_shape=[jax.ShapeDtypeStruct(values[0].shape, F32)]
        + [jax.ShapeDtypeStruct(value.shape, value.dtype) for value in through],
        input_output_aliases={count + i: 1 + i for i in range(len(through))},
        compiler_params=params(8),
        cost_estimate=cost(values[0].size * len(values), values[0].size * 4 * len(values)),
        name="add",
    )(*values, *after, *through)
    return outs if through else outs[0]


def prepare_kernel(slabs, incidence, row_weights, gain_map, gain_values, *rest):
    ahead, back, gains = rest[-6:-3]
    flat = rest[-1]
    angles, offsets, planes, block = row_weights.shape
    flat[...] = jnp.zeros_like(flat)
    slab = lax.axis_index("slab")
    for spot, offset in enumerate(order_of(offsets)):
        other = slab + offset - offsets // 2
        inside = jnp.where((other >= 0) & (other < slabs), 1, 0)
        for angle in range(angles):
            factor = (incidence[angle, 0, offset] * inside).astype(F32)
            at = (spot * angles + angle) * planes
            flat[at : at + planes, angle * block : (angle + 1) * block] = (
                row_weights[angle, offset] * factor
            )
    high, low = split(flat[...])
    back[...] = jnp.concatenate([high, low], axis=0)
    turned = flat[...].T
    high, low = split(turned)
    ahead[...] = jnp.concatenate([high, low, high], axis=1)
    lane = lax.broadcasted_iota(jnp.int32, (1, 2 * block), 1)
    first = lane < block
    blocks = gain_map.shape[1]
    for i in range(blocks // 2):
        low_gain = gain_values[gain_map[0, 2 * i]]
        high_gain = gain_values[gain_map[0, 2 * i + 1]]
        gains[:, 2 * i * block : 2 * (i + 1) * block] = jnp.where(first, low_gain, high_gain)


def prepare(incidence, row_weights, gain_map, gain_values, slabs, after, through):
    angles, offsets, planes, block = row_weights.shape
    rows = offsets * angles * planes
    columns = gain_map.shape[1] * block
    smem = pl.BlockSpec(memory_space=pltpu.SMEM)
    anywhere = pl.BlockSpec(memory_space=pl.ANY)
    vmem = pl.BlockSpec(memory_space=pltpu.VMEM)
    return pl.pallas_call(
        functools.partial(prepare_kernel, slabs),
        in_specs=[smem, vmem, smem, smem] + [anywhere] * (len(after) + len(through)),
        out_specs=[vmem] * 3 + [anywhere] * len(through),
        out_shape=[
            jax.ShapeDtypeStruct((angles * block, 3 * rows), BF16),
            jax.ShapeDtypeStruct((2 * rows, angles * block), BF16),
            jax.ShapeDtypeStruct((1, columns), F32),
        ]
        + [jax.ShapeDtypeStruct(value.shape, F32) for value in through],
        input_output_aliases={4 + len(after) + i: 3 + i for i in range(len(through))},
        scratch_shapes=[pltpu.VMEM((rows, angles * block), F32)],
        compiler_params=params(),
        cost_estimate=cost(1000000, 1 * MIB),
        name="prepare",
    )(incidence, row_weights, gain_map, gain_values, *after, *through)


def detector_kernel(offsets, ahead, back, gains, measured, *refs):
    lines = refs[:offsets]
    outs = refs[-1 - offsets : -1]
    sums = refs[-1]
    angles, block, width = measured.shape
    high, low = split(jnp.concatenate([line[...] for line in lines], axis=0))
    stacked = jnp.concatenate([high, high, low], axis=0)
    forward = jnp.dot(ahead[...], stacked, preferred_element_type=F32)
    gain = gains[...]
    residual = gain * forward - measured[...].reshape(angles * block, width)
    weighted = gain * residual
    cross = jnp.sum(residual * forward, axis=0, keepdims=True)
    energy = jnp.sum(forward * forward, axis=0, keepdims=True)
    sums[...] = jnp.concatenate([cross, energy], axis=0)
    high, low = split(weighted)
    count = back.shape[0] // 2
    main = jnp.dot(back[...], high, preferred_element_type=F32)
    planes = (
        main[:count] + main[count:] + jnp.dot(back[:count], low, preferred_element_type=F32)
    )
    size = count // offsets
    for offset in range(offsets):
        outs[offset][...] = planes[offset * size : (offset + 1) * size]


def detector(ahead, back, gains, measured, lines, after=(), steps=2):
    offsets = len(lines)
    angles, block, columns = measured.shape
    rows = lines[0].shape[0]
    width = columns // steps
    piece = pl.BlockSpec((rows, width), lambda i: (0, i))
    return pl.pallas_call(
        functools.partial(detector_kernel, offsets),
        grid=(steps,),
        in_specs=[
            full(ahead.shape),
            full(back.shape),
            pl.BlockSpec((1, width), lambda i: (0, i)),
            pl.BlockSpec((angles, block, width), lambda i: (0, 0, i)),
        ]
        + [piece] * offsets
        + [pl.BlockSpec(memory_space=pl.ANY)] * len(after),
        out_specs=[piece] * offsets + [pl.BlockSpec((2, width), lambda i: (0, i))],
        out_shape=[jax.ShapeDtypeStruct((rows, columns), F32)] * offsets
        + [jax.ShapeDtypeStruct((2, columns), F32)],
        compiler_params=params(),
        cost_estimate=cost(12 * angles * block * rows * offsets * columns // angles, 8 * MIB),
        name="detector",
    )(ahead, back, gains, measured, *lines, *after)


def group_kernel(blocks, sums, out):
    columns = sums.shape[1]
    block = columns // blocks
    mine = (
        lax.broadcasted_iota(jnp.int32, (blocks, columns), 1) // block
        == lax.broadcasted_iota(jnp.int32, (blocks, columns), 0)
    )
    cross = jnp.sum(jnp.where(mine, sums[0:1, :], 0.0), axis=1, keepdims=True)
    energy = jnp.sum(jnp.where(mine, sums[1:2, :], 0.0), axis=1, keepdims=True)
    row = lax.broadcasted_iota(jnp.int32, (blocks, 2 * blocks), 0)
    lane = lax.broadcasted_iota(jnp.int32, (blocks, 2 * blocks), 1)
    both = jnp.where(lane == row, cross, 0.0) + jnp.where(lane == row + blocks, energy, 0.0)
    out[...] = jnp.sum(both, axis=0, keepdims=True)


def group(sums, blocks):
    return pl.pallas_call(
        functools.partial(group_kernel, blocks),
        out_shape=jax.ShapeDtypeStruct((1, 2 * blocks), F32),
        compiler_params=params(),
        cost_estimate=cost(4 * blocks * sums.shape[1], MIB // 8),
        name="group",
    )(sums)


def spread_kernel(first, second, gain_map, *rest):
    out = rest[-1]
    blocks = gain_map.shape[1]
    index = gain_map[...].astype(F32)
    row = jnp.concatenate([first[...] + second[...], index, index], axis=1)
    out[...] = jnp.broadcast_to(row, out.shape)


def spread(first, second, gain_map, slabs, after):
    vmem = pl.BlockSpec(memory_space=pltpu.VMEM)
    return pl.pallas_call(
        spread_kernel,
        in_specs=[vmem] * 3 + [pl.BlockSpec(memory_space=pl.ANY)] * len(after),
        out_specs=vmem,
        out_shape=jax.ShapeDtypeStruct((slabs, 4 * gain_map.shape[1]), F32),
        compiler_params=params(),
        cost_estimate=cost(slabs * 256, MIB // 8),
        name="spread",
    )(first, second, gain_map, *after)


def gather_kernel(rows, gains, out, values, onehot):
    slabs = rows.shape[0]
    side = rows.shape[1] // 4
    height, width = out.shape
    half = slabs // 2
    whole = rows[...]

    def paired(at):
        part = whole[:, at * side : (at + 1) * side]
        return jnp.concatenate([part[:half], part[half:]], axis=1)

    index = paired(2).astype(jnp.int32)
    high = index // width
    low = index - high * width
    pieces = []
    for value in (paired(0), paired(1)):
        first = value.astype(BF16).astype(F32)
        second = (value - first).astype(BF16).astype(F32)
        pieces.append((first, second, value - first - second))
    row = lax.broadcasted_iota(jnp.int32, (height, 2 * side), 0)
    lane = lax.broadcasted_iota(jnp.int32, (width, 2 * side), 0)
    for p in range(half):
        run = slice(p * 2 * side, (p + 1) * 2 * side)
        onehot[:, run] = jnp.where(lane == low[p : p + 1], 1.0, 0.0).astype(BF16)
        mask = row == high[p : p + 1]
        for k in range(3):
            for kind in range(2):
                at = (2 * k + kind) * height
                piece = jnp.where(mask, pieces[kind][k][p : p + 1], 0.0)
                values[at : at + height, run] = piece.astype(BF16)
    parts = lax.dot_general(
        values[...], onehot[...], (((1,), (1,)), ((), ())), preferred_element_type=F32
    )
    total = parts[: 2 * height] + parts[2 * height : 4 * height] + parts[4 * height :]
    out[...] = gains[...] - total[:height] / (total[height:] + 1.0)


def gather(rows, gain_values):
    slabs = rows.shape[0]
    side = rows.shape[1] // 4
    width = 128
    height = gain_values.shape[0] // width
    return pl.pallas_call(
        gather_kernel,
        out_shape=jax.ShapeDtypeStruct((height, width), F32),
        scratch_shapes=[
            pltpu.VMEM((6 * height, slabs * side), BF16),
            pltpu.VMEM((width, slabs * side), BF16),
        ],
        compiler_params=params(),
        cost_estimate=cost(12 * height * width * slabs * side, MIB),
        name="gather",
    )(rows, gain_values.reshape(height, width)).reshape(-1)


def hand_kernel(*refs):
    del refs


def hand(value, after):
    anywhere = pl.BlockSpec(memory_space=pl.ANY)
    return pl.pallas_call(
        hand_kernel,
        in_specs=[anywhere] * 2,
        out_specs=anywhere,
        out_shape=jax.ShapeDtypeStruct(value.shape, value.dtype),
        input_output_aliases={0: 0},
        compiler_params=params(),
        cost_estimate=cost(0, 0),
        name="hand",
    )(value, after)


def smooth_kernel(slabs, volume, leading, trailing, *rest):
    out = rest[-1]
    planes, rows, columns = volume.shape
    swap = heading() > 0
    slab = lax.axis_index("slab")
    below = jnp.where(swap, trailing[...], leading[...])
    above = jnp.where(swap, leading[...], trailing[...])
    below = jnp.where(slab == 0, 0.0, below)
    above = jnp.where(slab == slabs - 1, 0.0, above)
    lane = lax.broadcasted_iota(jnp.int32, (rows, columns), 1)
    last = lane == columns - 1
    begin = lane == 0

    def fluxes(here, after):
        ahead = jnp.where(last, 0.0, pltpu.roll(here, columns - 1, 1))
        diff_z = after - here
        diff_u = ahead - here
        scale = lax.rsqrt(diff_z * diff_z + diff_u * diff_u + 0.25)
        return diff_z * scale, diff_u * scale

    flux_below, _ = fluxes(below, volume[0])
    for plane in range(planes):
        here = volume[plane]
        after = volume[plane + 1] if plane + 1 < planes else above
        flux_z, flux_u = fluxes(here, after)
        moved = jnp.where(begin, 0.0, pltpu.roll(flux_u, 1, 1))
        out[plane] = here - 0.2 * (flux_below - flux_z + moved - flux_u)
        flux_below = flux_z


def smooth(volume, leading, trailing, slabs, after):
    planes, depth, columns = volume.shape
    rows = 8
    block = pl.BlockSpec((planes, rows, columns), lambda i: (0, i, 0))
    edge = pl.BlockSpec((rows, columns), lambda i: (i, 0))
    return pl.pallas_call(
        functools.partial(smooth_kernel, slabs),
        grid=(depth // rows,),
        in_specs=[block, edge, edge] + [pl.BlockSpec(memory_space=pl.ANY)] * len(after),
        out_specs=block,
        out_shape=jax.ShapeDtypeStruct(volume.shape, F32),
        compiler_params=params(),
        cost_estimate=cost(40 * planes * depth * columns, 5 * MIB),
        name="smooth",
    )(volume, leading, trailing, *after)


def update_kernel(count, weights, base, *refs):
    images, out, turned = refs[:count], refs[-2], refs[-1]
    planes, depth, width = base.shape

    @pl.when(pl.program_id(0) == 0)
    def _():
        high, low = split(weights[...].T)
        turned[...] = jnp.concatenate([high, low, high], axis=1)

    high, low = split(jnp.concatenate([image[...] for image in images], axis=0))
    gradient = jnp.dot(
        turned[...], jnp.concatenate([high, high, low], axis=0), preferred_element_type=F32
    )
    out[...] = base[...] - 0.2 * gradient.reshape(planes, depth, width)


def update(weights, base, images, after=(), steps=2):
    planes, depth, columns = base.shape
    width = columns // steps
    rows = images[0].shape[0]
    block = pl.BlockSpec((planes, depth, width), lambda i: (0, 0, i))
    return pl.pallas_call(
        functools.partial(update_kernel, len(images)),
        grid=(steps,),
        in_specs=[full(weights.shape), block]
        + [pl.BlockSpec((rows, width), lambda i: (0, i))] * len(images)
        + [pl.BlockSpec(memory_space=pl.ANY)] * len(after),
        out_specs=block,
        out_shape=jax.ShapeDtypeStruct(base.shape, F32),
        scratch_shapes=[pltpu.VMEM((weights.shape[1], 3 * weights.shape[0]), BF16)],
        compiler_params=params(),
        cost_estimate=cost(6 * weights.size * columns, 5 * MIB),
        name="update",
    )(weights, base, *images, *after)


def local(volume, measured, incidence, row_weights, path_table, subset, gain_map, gain_values):
    slabs = lax.axis_size("slab")
    parts = lax.axis_size("ang")
    both = ("slab", "ang")

    def neighbours(turn):
        pairs = []
        for slab in range(slabs):
            for part in range(parts):
                target = slab + 1 - 2 * ((slab + turn) % 2)
                if 0 <= target < slabs:
                    pairs.append((slab * parts + part, target * parts + part))
                else:
                    pairs.append((slab * parts + part, slab * parts + (part ^ 1)))
        return pairs

    def flipped(bit):
        return [(i, i ^ bit) for i in range(slabs * parts)]

    def send(value, pairs):
        return lax.ppermute(value, both, pairs)

    first, second = neighbours(0), neighbours(1)
    mates, partners = flipped(1), flipped(2)

    mate_far, mate_near, far, near, weights, leading, trailing = make_lines(
        subset, path_table, volume
    )
    far = send(add(far, send(mate_far, mates)), partners)
    line = add(near, send(mate_near, mates), far)

    line_0 = send(line, first)
    line_1 = send(line, second)
    line_2 = send(line_0, second)
    line_3 = send(line_1, first)

    ahead, back, gains, leading, trailing = prepare(
        incidence,
        row_weights,
        gain_map,
        gain_values,
        slabs,
        (line_0, line_1),
        (leading, trailing),
    )
    leading = send(leading, first)
    trailing = send(trailing, second)

    *terms, sums = detector(
        ahead, back, gains, measured, (line_0, line_1, line_2, line_3, line)
    )
    to_first = send(terms[3], first)
    to_second = send(terms[2], second)

    totals = group(sums, gain_map.shape[1])
    totals = totals + send(totals, mates)
    to_second_next = add(terms[1], to_first, after=(totals,))
    to_first_next = add(terms[0], to_second, after=(totals,))
    other_totals = send(totals, partners)
    from_second = send(to_second_next, second)
    from_first = send(to_first_next, first)

    base = smooth(volume, leading, trailing, slabs, after=(to_first_next, to_second_next))
    own = add(terms[4], from_first, from_second, after=(other_totals, base))
    mate_own = send(own, mates)
    other = send(own, partners)

    rows = spread(totals, other_totals, gain_map, slabs, after=(mate_own,))
    rows = lax.all_to_all(rows, "slab", split_axis=0, concat_axis=0, tiled=True)
    other = hand(other, rows)
    mate_other = send(other, mates)
    gain_next = gather(rows, gain_values)

    volume_next = update(weights, base, (mate_other, mate_own, other, own))
    return volume_next, gain_next


def solution(mesh):
    in_specs = (
        P("slab", "ang", None),
        P("ang", "slab", None),
        P("ang", "slab", None),
        P("ang", None, None, None),
        P(None, "ang"),
        P(),
        P("slab", None),
        P(),
    )
    out_specs = (P("slab", "ang", None), P())
    return jax.shard_map(local, mesh=mesh, in_specs=in_specs, out_specs=out_specs, check_vma=False)
```
